32 devices in a mesh: sector: 4 (over y, core), row: 8 (over z, x).
Axes of the slice: x: 2, y: 2, z: 4, core: 2. Of those that a mesh axis runs over, the one named last changes fastest.
Arguments:
- amplitudes: bfloat16 [4096, 4, 8192], P('sector', None, 'row'), may hold values from -6 to 6
- next_site: bfloat16 [4, 4, 8192, 2048], P('sector', None, 'row'), may hold values from -0.03125 to 0.03125
- sector_rows: int32 [4], replicated, may hold values from 512 to 1024, as said below
- moves: int32 [2, 4], replicated, may hold values from 0 to 128, as said below
- angles: float32 [2, 4, 128], replicated, may hold values from -3.140625 to 3.140625
- ranks: int32 [4], replicated, may hold values from 256 to 1024, as said below
Outputs:
- canonical: bfloat16 [2048, 4096], P('row', 'sector')
The draws below stay inside these ranges and needn't reach their ends.
Inputs may be any that keep to these rules, and one draw needn't show every extreme that they name: `sector_rows`: one sector has exactly 1024 live rows and another exactly 512. `moves`: the entry of the last sector is 0, every other entry is 1 or more; for each gate some pair moves exactly 128 rows. `ranks`: each sector keeps at least half of its live rows and at most all of them; one sector keeps 1024 rows and one keeps 1024 // 4.
All inputs are finite; a program needn't handle non-finite values.
Results may differ from the reference program's by a relative error of at most 0.014.
Values may be sent and summed in bfloat16 or wider, within the bound.
A program may use at most 128 MiB of HBM per device.

```python
import math
import jax
import jax.numpy as jnp
from jax import lax

LSEC = 1024
PHYS = 4
RB = 8192
KOUT = 2048
MOVE = 128
SECTORS = 4


def sector_plan(key):
    keys = jax.random.split(jax.random.fold_in(key, 7), 5)
    sector_index = jnp.arange(SECTORS)
    center = SECTORS // 2
    live_rows = jax.random.randint(keys[0], (SECTORS,), LSEC // 2, LSEC + 1)
    smallest = jax.random.randint(keys[1], (), 0, SECTORS - 1)
    smallest = jnp.where(smallest >= center, smallest + 1, smallest)
    live_rows = jnp.where(sector_index == center, LSEC, live_rows)
    live_rows = jnp.where(sector_index == smallest, LSEC // 2, live_rows)
    spread = jax.random.randint(keys[2], (SECTORS,), 0, 1 << 20)
    kept_rows = live_rows // 2 + spread % (live_rows - live_rows // 2 + 1)
    kept_rows = jnp.where(sector_index == center, LSEC, kept_rows)
    kept_rows = jnp.where(sector_index == smallest, LSEC // 4, kept_rows)
    pair_rows = jax.random.randint(keys[3], (2, SECTORS), 1, MOVE + 1)
    fullest = jax.random.randint(keys[4], (2,), 0, SECTORS - 1)
    pair_rows = jnp.where(sector_index[None, :] == fullest[:, None], MOVE, pair_rows)
    pair_rows = jnp.where(sector_index[None, :] == SECTORS - 1, 0, pair_rows)
    return (live_rows.astype(jnp.int32), pair_rows.astype(jnp.int32), kept_rows.astype(jnp.int32))


def draw_sector_rows(key, part):
    return sector_plan(key)[0]


def draw_moves(key, part):
    return sector_plan(key)[1]


def draw_ranks(key, part):
    return sector_plan(key)[2]


def block_levels(rng, dims, shards, low, largest):
    def one(dim, parts):
        steps = jax.random.uniform(jax.random.fold_in(jax.random.fold_in(rng, 6), dim), (parts,), jnp.float32, low / len(shards), largest / len(shards))
        return jnp.repeat(jnp.exp(steps), dims[dim] // parts).reshape((-1,) + (1,) * (len(dims) - dim - 1))

    gain = one(*shards[0])
    for cut in shards[1:]:
        gain = gain * one(*cut)
    return gain


def bell_draw(own_key, dims, deviation, reach, cuts=(), held_as=jnp.bfloat16):
    array = jax.random.normal(own_key, dims, jnp.float32) * deviation
    if len(cuts) > 0:
        array = block_levels(own_key, dims, cuts, -0.22, 0.18) * array
    return jnp.clip(array, min=-reach, max=reach).astype(held_as)


def setup_inputs(seed: int = 0) -> dict:
    splits = jax.random.split(jax.random.key(seed), 7)
    amplitudes = bell_draw(splits[0], (SECTORS * LSEC, PHYS, RB), 1.0, 6.0, ((0, 4), (2, 8)))
    next_site = bell_draw(splits[1], (SECTORS, PHYS, RB, KOUT), (PHYS * RB) ** -0.5, 0.03125, ((0, 4), (2, 8)))
    sector_rows = draw_sector_rows(jax.random.fold_in(splits[6], 71), 0)
    moves = draw_moves(jax.random.fold_in(splits[6], 71), 0)
    angles = jnp.clip(jax.random.uniform(splits[4], (2, SECTORS, MOVE), jnp.float32, -3.140625, 3.140625), -3.140625, 3.140625)
    ranks = draw_ranks(jax.random.fold_in(splits[6], 71), 0)
    return {"amplitudes": amplitudes, "next_site": next_site, "sector_rows": sector_rows, "moves": moves, "angles": angles, "ranks": ranks}


def reference(amplitudes, next_site, sector_rows, moves, angles, ranks):
    blocks = amplitudes.astype(jnp.float32).reshape(SECTORS, LSEC, PHYS, RB)
    row_index = jnp.arange(LSEC)
    padded = []
    for sector in range(SECTORS):
        live_rows = jnp.where((row_index < sector_rows[sector])[:, None, None], blocks[sector], jnp.float32(0.0))
        padded.append(jnp.concatenate([live_rows, jnp.zeros((MOVE, PHYS, RB), jnp.float32)], 0))
    slot_index = jnp.arange(MOVE)
    for gate_index in range(2):
        for sector in range(SECTORS - 1):
            pair_count = moves[gate_index, sector]
            if gate_index == 0:
                start_a = (sector_rows[sector] - moves[0, sector]).astype(jnp.int32)
                start_b = jnp.int32(0)
            else:
                start_a = (sector_rows[sector] - moves[0, sector] - moves[1, sector]).astype(jnp.int32)
                start_b = moves[0, sector].astype(jnp.int32)
            rows_a = lax.dynamic_slice_in_dim(padded[sector], start_a, MOVE, 0)
            rows_b = lax.dynamic_slice_in_dim(padded[sector + 1], start_b, MOVE, 0)
            angle_row = angles[gate_index, sector][:, None, None]
            valid = (slot_index < pair_count)[:, None, None]
            new_a = jnp.where(valid, jnp.cos(angle_row) * rows_a - jnp.sin(angle_row) * rows_b, rows_a)
            new_b = jnp.where(valid, jnp.sin(angle_row) * rows_a + jnp.cos(angle_row) * rows_b, rows_b)
            padded[sector] = lax.dynamic_update_slice_in_dim(padded[sector], new_a, start_a, 0)
            padded[sector + 1] = lax.dynamic_update_slice_in_dim(padded[sector + 1], new_b, start_b, 0)
    results = []
    for sector in range(SECTORS):
        block_rows = padded[sector][:LSEC].astype(jnp.bfloat16)
        contracted = jnp.einsum('prk,lpr->kl', next_site[sector].astype(jnp.float32), block_rows.astype(jnp.float32), precision=lax.Precision.HIGHEST).astype(jnp.bfloat16)
        wide_rows = contracted.astype(jnp.float32)
        dead_rows = (row_index >= sector_rows[sector]).astype(jnp.float32)
        gram_matrix = jnp.dot(wide_rows.T, wide_rows, precision=lax.Precision.HIGHEST) + jnp.diag(dead_rows)
        factor_low = jnp.linalg.cholesky(gram_matrix)
        solved = jax.scipy.linalg.solve_triangular(factor_low, wide_rows.T, lower=True).T
        kept_mask = ((row_index >= sector_rows[sector] - ranks[sector]) & (row_index < sector_rows[sector])).astype(jnp.float32)
        results.append((solved * math.sqrt(KOUT) * kept_mask[None, :]).astype(jnp.bfloat16))
    return jnp.concatenate(results, 1)
```

```python
import math

import jax
import jax.numpy as jnp
from jax import lax
from jax.experimental import pallas as pl
from jax.experimental.pallas import tpu as pltpu
from jax.sharding import PartitionSpec as P

KOUT = 2048


def shifted(x, axis, by):
    size = lax.axis_size(axis)
    pairs = [(i, i + by) for i in range(size) if 0 <= i + by < size]
    return lax.ppermute(x, axis, pairs)


TILE = 128
GROUP = 4


def rotate_rows(padded, start, here, other, angle, count, sign):
    slot_index = jnp.arange(here.shape[0])
    mine = here.astype(jnp.float32)
    cos = jnp.cos(angle)[:, None, None]
    sin = sign * jnp.sin(angle)[:, None, None]
    rotated = (cos * mine + sin * other.astype(jnp.float32)).astype(jnp.bfloat16)
    rows = lax.dynamic_slice_in_dim(padded, start, here.shape[0], 0)
    rows = jnp.where((slot_index < count)[:, None, None], rotated, rows)
    return lax.dynamic_update_slice_in_dim(padded, rows, start, 0)


def inverse_factor(tile):
    slabs = TILE // 8
    lane = lax.broadcasted_iota(jnp.int32, (8, TILE), 1)
    sub = lax.broadcasted_iota(jnp.int32, (8, TILE), 0)
    a = [tile[8 * i : 8 * i + 8] for i in range(slabs)]
    for first in range(0, TILE, GROUP):
        top = first // 8
        cols = [
            {i: jnp.broadcast_to(a[i][:, first + q : first + q + 1], (8, TILE)) for i in range(top, slabs)}
            for q in range(GROUP)
        ]
        for q in range(GROUP):
            j = first + q
            r = j - 8 * top
            inv = 1.0 / cols[q][top][r : r + 1]
            row = a[top][r : r + 1]
            heads = {p: cols[p][top][r : r + 1] for p in range(q + 1, GROUP)}
            for i in range(top, slabs):
                m = cols[q][i] * inv
                hit = lane == j
                if i == top:
                    m = jnp.where(sub > r, m, 0.0)
                    hit = hit & (sub > r)
                for p in range(q + 1, GROUP):
                    cols[p][i] = cols[p][i] - m * heads[p]
                a[i] = jnp.where(hit, -m, a[i] - m * row)
    out = []
    for i in range(slabs):
        on = lane == sub + 8 * i
        pivot = jnp.sum(jnp.where(on, a[i], 0.0), axis=1, keepdims=True)
        unit = jnp.where(lane < sub + 8 * i, a[i], jnp.where(on, 1.0, 0.0))
        out.append(unit * lax.rsqrt(pivot))
    return jnp.concatenate(out, 0)


def dot_full(x, y, dims):
    return lax.dot_general(
        x, y, (dims, ((), ())), precision=lax.Precision.HIGHEST, preferred_element_type=jnp.float32
    )


def whiten_kernel(gram_ref, cols_ref, scale_ref, out_ref, work, rest, panel):
    size = work.shape[0]
    blocks = size // TILE
    work[...] = gram_ref[...]
    rest[...] = cols_ref[...].astype(jnp.float32)

    def block_step(k, carry):
        at = pl.ds(pl.multiple_of(k * TILE, TILE), TILE)
        inverse = inverse_factor(work[at, at])
        solved = dot_full(rest[:, at], inverse, ((1,), (1,)))
        out_ref[:, at] = (solved * scale_ref[:, at]).astype(jnp.bfloat16)
        panel[...] = dot_full(inverse, work[at, :], ((1,), (0,)))

        def trail(i, inner):
            to = pl.ds(pl.multiple_of(i * TILE, TILE), TILE)
            part = panel[:, to]
            work[to, :] = work[to, :] - dot_full(part.T, panel[...], ((1,), (0,)))
            rest[:, to] = rest[:, to] - dot_full(solved, part, ((1,), (0,)))
            return inner

        return lax.fori_loop(k + 1, blocks, trail, carry)

    lax.fori_loop(0, blocks, block_step, 0)


def whiten(gram_matrix, contracted, scale):
    rows, size = contracted.shape
    vmem = pl.BlockSpec(memory_space=pltpu.VMEM)
    return pl.pallas_call(
        whiten_kernel,
        out_shape=jax.ShapeDtypeStruct((rows, size), jnp.bfloat16),
        in_specs=[vmem] * 3,
        out_specs=vmem,
        scratch_shapes=[
            pltpu.VMEM((size, size), jnp.float32),
            pltpu.VMEM((rows, size), jnp.float32),
            pltpu.VMEM((TILE, size), jnp.float32),
        ],
        compiler_params=pltpu.CompilerParams(vmem_limit_bytes=40 * 1024 * 1024),
    )(gram_matrix, contracted, scale)


def per_device(amplitudes, next_site, sector_rows, moves, angles, ranks):
    sector_id = lax.axis_index("sector")
    sector_rows_count = amplitudes.shape[0]
    move_rows = sector_rows_count // 8
    row_index = jnp.arange(sector_rows_count)
    live_rows = sector_rows[sector_id]
    prev_id = jnp.maximum(sector_id - 1, 0)
    count_here = moves[:, sector_id]
    count_prev = jnp.where(sector_id > 0, moves[:, prev_id], 0)
    local_rows = jnp.where((row_index < live_rows)[:, None, None], amplitudes, jnp.bfloat16(0))
    padded = jnp.pad(local_rows, ((0, move_rows), (0, 0), (0, 0)))
    starts_a = [live_rows - count_here[0], live_rows - count_here[0] - count_here[1]]
    starts_b = [jnp.int32(0), count_prev[0]]
    ends_a = [lax.dynamic_slice_in_dim(padded, at, move_rows, 0) for at in starts_a]
    ends_b = [lax.dynamic_slice_in_dim(padded, at, move_rows, 0) for at in starts_b]
    from_below = shifted(jnp.concatenate(ends_a, 0), "sector", 1)
    from_above = shifted(jnp.concatenate(ends_b, 0), "sector", -1)
    for gate in range(2):
        part = slice(gate * move_rows, (gate + 1) * move_rows)
        padded = rotate_rows(
            padded, starts_a[gate], ends_a[gate], from_above[part],
            angles[gate][sector_id], count_here[gate], -1.0,
        )
        padded = rotate_rows(
            padded, starts_b[gate], ends_b[gate], from_below[part],
            angles[gate][prev_id], count_prev[gate], 1.0,
        )
    block_rows = padded[:sector_rows_count]
    partial = jnp.einsum(
        "prk,lpr->kl", next_site[0], block_rows, preferred_element_type=jnp.float32
    ).astype(jnp.bfloat16)
    contracted = lax.psum_scatter(partial, "row", scatter_dimension=0, tiled=True)
    gathered = lax.all_gather(contracted, "row", axis=0, tiled=True)
    gram_matrix = lax.dot_general(
        gathered, gathered, (((0,), (0,)), ((), ())), preferred_element_type=jnp.float32
    )
    gram_matrix = gram_matrix + jnp.diag((row_index >= live_rows).astype(jnp.float32))
    kept = (row_index >= live_rows - ranks[sector_id]) & (row_index < live_rows)
    scale = jnp.where(kept, jnp.float32(math.sqrt(KOUT)), 0.0)[None, :]
    return whiten(gram_matrix, contracted, scale)


def solution(mesh):
    placed = (P("sector", None, "row"), P("sector", None, "row", None), P(), P(), P(), P())
    return jax.shard_map(
        per_device, mesh=mesh, in_specs=placed, out_specs=P("row", "sector"), check_vma=False
    )
```

```python
import math

import jax
import jax.numpy as jnp
from jax import lax
from jax.experimental import pallas as pl
from jax.experimental.pallas import tpu as pltpu
from jax.sharding import PartitionSpec as P

KOUT = 2048


def shifted(x, axis, by):
    size = lax.axis_size(axis)
    pairs = [(i, i + by) for i in range(size) if 0 <= i + by < size]
    return lax.ppermute(x, axis, pairs)


TILE = 128
GROUP = 4


def rotate_rows(padded, start, here, other, angle, count, sign):
    slot_index = jnp.arange(here.shape[0])
    mine = here.astype(jnp.float32)
    cos = jnp.cos(angle)[:, None, None]
    sin = sign * jnp.sin(angle)[:, None, None]
    rotated = (cos * mine + sin * other.astype(jnp.float32)).astype(jnp.bfloat16)
    rows = jnp.where((slot_index < count)[:, None, None], rotated, here)
    return lax.dynamic_update_slice_in_dim(padded, rows, start, 0)


def inverse_factor(tile):
    slabs = TILE // 8
    lane = lax.broadcasted_iota(jnp.int32, (8, TILE), 1)
    sub = lax.broadcasted_iota(jnp.int32, (8, TILE), 0)
    a = [tile[8 * i : 8 * i + 8] for i in range(slabs)]
    for first in range(0, TILE, GROUP):
        top = first // 8
        cols = [
            {i: jnp.broadcast_to(a[i][:, first + q : first + q + 1], (8, TILE)) for i in range(top, slabs)}
            for q in range(GROUP)
        ]
        for q in range(GROUP):
            j = first + q
            r = j - 8 * top
            inv = 1.0 / cols[q][top][r : r + 1]
            row = a[top][r : r + 1]
            heads = {p: cols[p][top][r : r + 1] for p in range(q + 1, GROUP)}
            for i in range(top, slabs):
                m = cols[q][i] * inv
                hit = lane == j
                if i == top:
                    m = jnp.where(sub > r, m, 0.0)
                    hit = hit & (sub > r)
                for p in range(q + 1, GROUP):
                    cols[p][i] = cols[p][i] - m * heads[p]
                a[i] = jnp.where(hit, -m, a[i] - m * row)
    out = []
    for i in range(slabs):
        on = lane == sub + 8 * i
        pivot = jnp.sum(jnp.where(on, a[i], 0.0), axis=1, keepdims=True)
        unit = jnp.where(lane < sub + 8 * i, a[i], jnp.where(on, 1.0, 0.0))
        out.append(unit * lax.rsqrt(pivot))
    return jnp.concatenate(out, 0)


def dot_full(x, y, dims):
    return lax.dot_general(
        x, y, (dims, ((), ())), precision=lax.Precision.HIGHEST, preferred_element_type=jnp.float32
    )


def whiten_kernel(gram_ref, cols_ref, scale_ref, out_ref, work, rest, panel):
    size = work.shape[0]
    blocks = size // TILE
    work[...] = gram_ref[...]
    rest[...] = cols_ref[...].astype(jnp.float32)

    def block_step(k, carry):
        at = pl.ds(pl.multiple_of(k * TILE, TILE), TILE)
        inverse = inverse_factor(work[at, at])
        solved = dot_full(rest[:, at], inverse, ((1,), (1,)))
        out_ref[:, at] = (solved * scale_ref[:, at]).astype(jnp.bfloat16)
        panel[...] = dot_full(inverse, work[at, :], ((1,), (0,)))

        def trail(i, inner):
            to = pl.ds(pl.multiple_of(i * TILE, TILE), TILE)
            part = panel[:, to]
            work[to, :] = work[to, :] - dot_full(part.T, panel[...], ((1,), (0,)))
            rest[:, to] = rest[:, to] - dot_full(solved, part, ((1,), (0,)))
            return inner

        return lax.fori_loop(k + 1, blocks, trail, carry)

    lax.fori_loop(0, blocks, block_step, 0)


def whiten(gram_matrix, contracted, scale):
    rows, size = contracted.shape
    vmem = pl.BlockSpec(memory_space=pltpu.VMEM)
    return pl.pallas_call(
        whiten_kernel,
        out_shape=jax.ShapeDtypeStruct((rows, size), jnp.bfloat16),
        in_specs=[vmem] * 3,
        out_specs=vmem,
        scratch_shapes=[
            pltpu.VMEM((size, size), jnp.float32),
            pltpu.VMEM((rows, size), jnp.float32),
            pltpu.VMEM((TILE, size), jnp.float32),
        ],
        compiler_params=pltpu.CompilerParams(vmem_limit_bytes=40 * 1024 * 1024),
    )(gram_matrix, contracted, scale)


def per_device(amplitudes, next_site, sector_rows, moves, angles, ranks):
    sector_id = lax.axis_index("sector")
    sector_rows_count = amplitudes.shape[0]
    move_rows = sector_rows_count // 8
    row_index = jnp.arange(sector_rows_count)
    live_rows = sector_rows[sector_id]
    prev_id = jnp.maximum(sector_id - 1, 0)
    count_here = moves[:, sector_id]
    count_prev = jnp.where(sector_id > 0, moves[:, prev_id], 0)
    wide_rows = jnp.pad(amplitudes, ((0, move_rows), (0, 0), (0, 0)))
    wide_index = jnp.arange(sector_rows_count + move_rows)
    padded = jnp.where((wide_index < live_rows)[:, None, None], wide_rows, jnp.bfloat16(0))
    starts_a = [live_rows - count_here[0], live_rows - count_here[0] - count_here[1]]
    starts_b = [jnp.int32(0), count_prev[0]]
    ends_a = [lax.dynamic_slice_in_dim(padded, at, move_rows, 0) for at in starts_a]
    ends_b = [lax.dynamic_slice_in_dim(padded, at, move_rows, 0) for at in starts_b]
    from_below = shifted(jnp.concatenate(ends_a, 0), "sector", 1)
    from_above = shifted(jnp.concatenate(ends_b, 0), "sector", -1)
    for gate in (1, 0):
        part = slice(gate * move_rows, (gate + 1) * move_rows)
        padded = rotate_rows(
            padded, starts_a[gate], ends_a[gate], from_above[part],
            angles[gate][sector_id], count_here[gate], -1.0,
        )
    for gate in (0, 1):
        part = slice(gate * move_rows, (gate + 1) * move_rows)
        padded = rotate_rows(
            padded, starts_b[gate], ends_b[gate], from_below[part],
            angles[gate][prev_id], count_prev[gate], 1.0,
        )
    block_rows = padded[:sector_rows_count]
    partial = jnp.einsum(
        "prk,lpr->kl", next_site[0], block_rows, preferred_element_type=jnp.float32
    ).astype(jnp.bfloat16)
    contracted = lax.psum_scatter(partial, "row", scatter_dimension=0, tiled=True)
    gathered = lax.all_gather(contracted, "row", axis=0, tiled=True)
    gram_matrix = lax.dot_general(
        gathered, gathered, (((0,), (0,)), ((), ())), preferred_element_type=jnp.float32
    )
    gram_matrix = gram_matrix + jnp.diag((row_index >= live_rows).astype(jnp.float32))
    kept = (row_index >= live_rows - ranks[sector_id]) & (row_index < live_rows)
    scale = jnp.where(kept, jnp.float32(math.sqrt(KOUT)), 0.0)[None, :]
    return whiten(gram_matrix, contracted, scale)


def solution(mesh):
    placed = (P("sector", None, "row"), P("sector", None, "row", None), P(), P(), P(), P())
    return jax.shard_map(
        per_device, mesh=mesh, in_specs=placed, out_specs=P("row", "sector"), check_vma=False
    )
```
